768 devices in a mesh: aa: 12 (over z_lo, core), ba: 64 (over z_hi, y, x).
Axes of the slice: x: 4, y: 8, z: 12 (z_hi: 2, z_lo: 6; z = z_hi * 6 + z_lo), core: 2. Of those that a mesh axis runs over, the one named last changes fastest.
Arguments:
- activations: bfloat16 [3072, 4224], P('aa', 'ba'), may hold values from -16 to 16
- out_grad: bfloat16 [3072, 4096], P('aa', 'ba'), may hold values from -0.107910156 to 0.107910156
- momentum: float32 [4224, 4096], P('aa', 'ba'), may hold values from -6 to 6
- weight: float32 [4224, 4096], P('aa', 'ba'), may hold values from -6 to 6
- norm_scale: float32 [], replicated, may hold values from 128.99231 to 257.98462
- step_size: float32 [], replicated, may hold values from 0.5 to 2
Outputs:
- new_weight: float32 [4224, 4096], P('aa', 'ba')
- new_momentum: float32 [4224, 4096], P('aa', 'ba')
The draws below stay inside these ranges and needn't reach their ends.
All inputs are finite; a program needn't handle non-finite values.
Results may differ from the reference program's by a relative error of at most 0.00068.
Values may be sent and summed in bfloat16 or wider, within the bound.
No kernel may reach another device: no remote copies, remote signals or barrier semaphores. Data moves between devices by JAX's collectives and lax.ppermute only.
A program may use at most 32 MiB of HBM per device.

```python
import math
import jax
import jax.numpy as jnp

ROWS = 4224
COLS = 4096
TOKENS = 3072


def strengthened(result, own_key, source, target, shards_of, factor):
    owner, partner = [(jnp.arange(result.shape[position]) // (result.shape[position] // shards_of)).reshape([-1 if axis == position else 1 for axis in range(result.ndim)]) for position in (source, target)]
    chosen = jax.random.permutation(own_key, shards_of)[partner]
    strong = (owner == chosen) | (owner == (partner + shards_of // 2) % shards_of)
    return jnp.where(strong, factor * result, result)


def steps_of(own_key, extent, cuts, least, high):
    level, own = 1.0, jax.random.fold_in(own_key, 6)
    for position, blocks in cuts:
        heights = jnp.exp(jax.random.uniform(jax.random.fold_in(own, position), (blocks,), jnp.float32, least / len(cuts), high / len(cuts)))
        level = level * jnp.repeat(heights, extent[position] // blocks).reshape([-1 if axis == position else 1 for axis in range(len(extent))])
    return level


def normal_values(own_key, shape, width, most, split=(), kind=jnp.bfloat16):
    array = width * jax.random.normal(own_key, shape, jnp.float32)
    if split:
        array = array * steps_of(own_key, shape, split, -0.22, 0.18)
    return jnp.clip(array, -most, most).astype(kind)


def gaussian_with(own_key, extent, width, limit, pieces, heavy, kind=jnp.bfloat16):
    drawn = width * jax.random.normal(own_key, extent, jnp.float32)
    if pieces:
        drawn = drawn * steps_of(own_key, extent, pieces, -0.22, 0.18)
    return jnp.clip(strengthened(drawn, jax.random.fold_in(own_key, 3), *heavy), -limit, limit).astype(kind)


def setup_inputs(seed: int = 0) -> dict:
    key_of = jax.random.split(jax.random.key(seed), 7)
    return {
        "activations": gaussian_with(key_of[0], (TOKENS, ROWS), 1.0, 16.0, ((0, 12), (1, 64)), (0, 1, 64, 4.0)),
        "out_grad": normal_values(key_of[1], (TOKENS, COLS), (TOKENS ** -0.5), 0.107910156, ((0, 12), (1, 64))),
        "momentum": normal_values(key_of[2], (ROWS, COLS), 1.0, 6.0, ((0, 12), (1, 64)), jnp.float32),
        "weight": normal_values(key_of[3], (ROWS, COLS), 1.0, 6.0, ((0, 12), (1, 64)), jnp.float32),
        "norm_scale": jnp.clip(jnp.exp(jax.random.uniform(key_of[4], (), jnp.float32, math.log(128.99231), math.log(257.98462))), 128.99231, 257.98462),
        "step_size": jnp.clip(jnp.exp(jax.random.uniform(key_of[5], (), jnp.float32, math.log(0.5), math.log(2.0))), 0.5, 2.0),
    }


def reference(activations, out_grad, momentum, weight, norm_scale, step_size):
    gradient = jnp.dot(activations.T, out_grad, preferred_element_type=jnp.float32)
    new_momentum = 0.95 * momentum + gradient
    scaled = (new_momentum / norm_scale).astype(jnp.bfloat16)
    gram = jnp.dot(scaled.T, scaled, preferred_element_type=jnp.float32).astype(jnp.bfloat16)
    first_power = jnp.dot(scaled, gram, preferred_element_type=jnp.float32).astype(jnp.bfloat16)
    second_power = jnp.dot(first_power, gram, preferred_element_type=jnp.float32)
    direction = 3.4445 * scaled.astype(jnp.float32) - 4.775 * first_power.astype(jnp.float32) + 2.0315 * second_power
    factor = 0.2 * math.sqrt(max(ROWS, COLS))
    new_weight = weight - step_size * factor * direction
    return (new_weight, new_momentum)
```

```python
import math

import jax
import jax.numpy as jnp
from jax import lax
from jax.sharding import Mesh
from jax.sharding import PartitionSpec as P

ROWS = 4224
COLS = 4096
ZL, CORES, ZH, Y, X = 6, 2, 2, 8, 4
COLUMN = ("zl", "core", "zh")
SWAP = [(0, 1), (1, 0)]


def place(zl, core, zh):
    return (zl * CORES + core) * ZH + zh


TO_WORK = [
    (place(3 * zh + zl // 2, zl % 2, core), place(zl, core, zh))
    for zl in range(ZL)
    for core in range(CORES)
    for zh in range(ZH)
]
TO_HOME = [(work, home) for home, work in TO_WORK]


def contract(left, right, dims):
    return lax.dot_general(left, right, (dims, ((), ())), preferred_element_type=jnp.float32)


def exchanged(pieces, axes):
    return lax.all_to_all(pieces, axes, split_axis=0, concat_axis=0, tiled=True)


def from_all(shard, axes, size):
    return exchanged(jnp.broadcast_to(shard[None], (size, *shard.shape)), axes)


def over_plane(tile):
    rows, width = tile.shape
    by_y = from_all(tile, "y", Y).reshape(Y * rows, width)
    return from_all(by_y, "x", X).reshape(X * Y * rows, width)


def per_device(activations, out_grad, momentum, weight, norm_scale, step_size):
    own_half = lax.axis_index("core") == lax.axis_index("zh")
    act, grad_out = activations.T, out_grad.T
    features, tokens = act.shape
    peer_out = lax.ppermute(grad_out, "zh", SWAP)
    kept = lax.ppermute(momentum.T, COLUMN, TO_WORK)

    act = over_plane(act).reshape(X, Y, features, tokens)
    act = act.transpose(1, 0, 2, 3).reshape(ZL, -1, tokens)
    mine = jnp.where(own_half, grad_out, peer_out)
    other = jnp.where(own_half, peer_out, grad_out)
    leaving = jnp.stack([contract(other, act[k], ((1,), (1,))) for k in range(ZL)])
    came = lax.ppermute(leaving, "core", SWAP)
    staying = jnp.stack([contract(mine, act[k], ((1,), (1,))) for k in range(ZL)])
    gradient = exchanged(staying + came, "zl").sum(axis=0)

    new_momentum = 0.95 * kept + gradient
    scaled = (new_momentum / norm_scale).astype(jnp.bfloat16)
    momentum_home = lax.ppermute(new_momentum, COLUMN, TO_HOME).T

    width = scaled.shape[0]
    pair = jnp.concatenate([scaled, lax.ppermute(scaled, "core", SWAP)])
    panel = over_plane(scaled)
    depth = panel.shape[0]
    share = -(-depth // (ZL * ZH * 16)) * 16
    part = contract(panel, pair, ((1,), (1,)))
    part = jnp.pad(part, ((0, ZL * ZH * share - depth), (0, 0)))
    part = part.reshape(ZL * ZH, share, 2 * width)
    gram = exchanged(part, ("zh", "zl")).sum(axis=0).astype(jnp.bfloat16)
    gram = from_all(gram, ("zh", "zl"), ZL * ZH).reshape(-1, 2 * width)[:depth]

    def times_gram(rows):
        both = contract(gram, rows, ((0,), (0,)))
        return both[:width] + lax.ppermute(both[width:], "core", SWAP)

    first_power = times_gram(panel).astype(jnp.bfloat16)
    second_power = times_gram(over_plane(first_power))
    direction = (
        3.4445 * scaled.astype(jnp.float32)
        - 4.775 * first_power.astype(jnp.float32)
        + 2.0315 * second_power
    )
    direction = lax.ppermute(direction, COLUMN, TO_HOME).T
    factor = 0.2 * math.sqrt(max(ROWS, COLS))
    return (weight - step_size * factor * direction, momentum_home)


def solution(mesh):
    torus = Mesh(
        mesh.devices.reshape(ZL, CORES, ZH, Y, X), ("zl", "core", "zh", "y", "x")
    )
    tiles = P(("zl", "core"), ("zh", "y", "x"))
    return jax.shard_map(
        per_device,
        mesh=torus,
        in_specs=(tiles, tiles, tiles, tiles, P(), P()),
        out_specs=(tiles, tiles),
        check_vma=False,
    )
```

```python
import math

import jax
import jax.numpy as jnp
from jax import lax
from jax.sharding import Mesh
from jax.sharding import PartitionSpec as P

ROWS = 4224
COLS = 4096
Z1, Z0, CORES, ZH, Y, X = 3, 2, 2, 2, 8, 4
AXES = ("z1", "z0", "core", "zh", "y", "x")
COLUMN = ("z1", "z0", "core", "zh")
RING = ("zh", "z1", "z0")
NEAR = ("z1", "z0", "zh")
ZL, Z = Z1 * Z0, ZH * Z1 * Z0


def place(zl, core, zh):
    return (zl * CORES + core) * ZH + zh


TO_WORK = [
    (place(3 * zh + zl // 2, zl % 2, core), place(zl, core, zh))
    for zl in range(ZL)
    for core in range(CORES)
    for zh in range(ZH)
]
TO_HOME = [(work, home) for home, work in TO_WORK]


def ring(z):
    return z % Z % ZL * ZH + z % Z // ZL


EVEN_PAIRS = [(ring(z), ring(z ^ 1)) for z in range(Z)]
ODD_PAIRS = [(ring(z), ring((z - 1 ^ 1) + 1)) for z in range(Z)]


def contract(left, right, dims):
    return lax.dot_general(left, right, (dims, ((), ())), preferred_element_type=jnp.float32)


def exchanged(pieces, axes):
    return lax.all_to_all(pieces, axes, split_axis=0, concat_axis=0, tiled=True)


def from_all(shard, axes, size):
    return exchanged(jnp.broadcast_to(shard[None], (size, *shard.shape)), axes)


def over_plane(tile):
    rows, width = tile.shape
    by_y = from_all(tile, "y", Y).reshape(Y * rows, width)
    return from_all(by_y, "x", X).reshape(X * Y * rows, width)


def per_device(activations, out_grad, momentum, weight, norm_scale, step_size):
    core, high, odd = (lax.axis_index(name) for name in ("core", "zh", "z0"))
    act, grad_out = activations.T, out_grad.T
    features, tokens = act.shape
    peer_out = lax.ppermute(grad_out, "zh", [(0, 1), (1, 0)])
    kept = lax.ppermute(momentum.T, COLUMN, TO_WORK)

    act = over_plane(act).reshape(X, Y, features, tokens)
    act = act.transpose(1, 0, 2, 3).reshape(ZL, -1, tokens)
    low_half = jnp.where(high == 0, grad_out, peer_out)
    high_half = jnp.where(high == 0, peer_out, grad_out)
    part = jnp.stack(
        [contract(half, act[k], ((1,), (1,))) for half in (low_half, high_half) for k in range(ZL)]
    )
    width, height = part.shape[1:]
    part = exchanged(part.reshape(CORES, ZL, width, height), "core").sum(axis=0)
    part = part.reshape(Z1, Z0, width, height).transpose(1, 0, 2, 3)
    part = exchanged(part, "z0").sum(axis=0)
    gradient = exchanged(part, "z1").sum(axis=0)

    new_momentum = 0.95 * kept + gradient
    scaled = (new_momentum / norm_scale).astype(jnp.bfloat16)
    momentum_home = lax.ppermute(new_momentum, COLUMN, TO_HOME)

    pair = lax.all_gather(scaled, "core", axis=0, tiled=True)
    panel = over_plane(scaled)
    panel, momentum_home = lax.optimization_barrier((panel, momentum_home))
    depth = panel.shape[0]
    part = contract(panel, pair, ((1,), (1,)))
    piece = -(-depth // (2 * Z * 8)) * 8
    part = jnp.pad(part, ((0, 2 * Z * piece - depth), (0, 0)))
    part = part.reshape(2, Z0, Z // Z0 * piece, CORES * width)
    leaving = lax.dynamic_index_in_dim(part, 1 - odd, 1, False)
    staying = lax.dynamic_index_in_dim(part, odd, 1, False)
    came = jnp.stack(
        [lax.ppermute(leaving[0], NEAR, EVEN_PAIRS), lax.ppermute(leaving[1], NEAR, ODD_PAIRS)]
    )
    part = (staying + came).reshape(2, Z // Z0, piece, CORES * width).transpose(1, 0, 2, 3)
    gram = exchanged(part, ("zh", "z1")).sum(axis=0).astype(jnp.bfloat16)
    gram = from_all(gram, RING, Z).reshape(Z // Z0, Z0, 2, piece, CORES * width)
    gram = gram.transpose(2, 1, 0, 3, 4).reshape(-1, CORES * width)[:depth]

    def times_gram(rows):
        both = contract(gram, rows, ((0,), (0,))).reshape(CORES, width, height)
        both = lax.all_gather(both, "core", axis=0, tiled=False)
        return lax.dynamic_index_in_dim(both, core, 1, False).sum(axis=0)

    first_power = times_gram(panel).astype(jnp.bfloat16)
    second_power = times_gram(over_plane(first_power))
    direction = (
        3.4445 * scaled.astype(jnp.float32)
        - 4.775 * first_power.astype(jnp.float32)
        + 2.0315 * second_power
    )
    direction = lax.ppermute(direction, COLUMN, TO_HOME).T
    factor = 0.2 * math.sqrt(max(ROWS, COLS))
    return (weight - step_size * factor * direction, momentum_home.T)


def solution(mesh):
    torus = Mesh(mesh.devices.reshape(Z1, Z0, CORES, ZH, Y, X), AXES)
    tiles = P(("z1", "z0", "core"), ("zh", "y", "x"))
    return jax.shard_map(
        per_device,
        mesh=torus,
        in_specs=(tiles, tiles, tiles, tiles, P(), P()),
        out_specs=(tiles, tiles),
        check_vma=False,
    )
```

```python
import math

import jax
import jax.numpy as jnp
from jax import lax
from jax.experimental.layout import Layout, with_layout_constraint
from jax.sharding import Mesh
from jax.sharding import PartitionSpec as P

ROWS = 4224
COLS = 4096
Z1, Z0, CORES, ZH, Y, X = 3, 2, 2, 2, 8, 4
AXES = ("z1", "z0", "core", "zh", "y", "x")
COLUMN = ("z1", "z0", "core", "zh")
RING = ("zh", "z1", "z0")
NEAR = ("z1", "z0", "zh")
ZL, Z = Z1 * Z0, ZH * Z1 * Z0


def place(zl, core, zh):
    return (zl * CORES + core) * ZH + zh


TO_WORK = [
    (place(3 * zh + zl // 2, zl % 2, core), place(zl, core, zh))
    for zl in range(ZL)
    for core in range(CORES)
    for zh in range(ZH)
]
TO_HOME = [(work, home) for home, work in TO_WORK]


def ring(z):
    return z % Z % ZL * ZH + z % Z // ZL


EVEN_PAIRS = [(ring(z), ring(z ^ 1)) for z in range(Z)]
ODD_PAIRS = [(ring(z), ring((z - 1 ^ 1) + 1)) for z in range(Z)]


def contract(left, right, dims):
    return lax.dot_general(left, right, (dims, ((), ())), preferred_element_type=jnp.float32)


def exchanged(pieces, axes):
    return lax.all_to_all(pieces, axes, split_axis=0, concat_axis=0, tiled=True)


def from_all(shard, axes, size):
    return exchanged(jnp.broadcast_to(shard[None], (size, *shard.shape)), axes)


def row_major(array):
    return with_layout_constraint(array, Layout(tuple(range(array.ndim))))


def over_plane(tile, beside_y=(), beside_x=()):
    rows, width = tile.shape
    by_y = from_all(tile, "y", Y).reshape(Y * rows, width)
    by_y, *beside_y = lax.optimization_barrier((row_major(by_y), *beside_y))
    panel = from_all(by_y, "x", X).reshape(X * Y * rows, width)
    panel, *beside_x = lax.optimization_barrier((row_major(panel), *beside_x))
    return panel, *beside_y, *beside_x


def per_device(activations, out_grad, momentum, weight, norm_scale, step_size):
    core, high, odd = (lax.axis_index(name) for name in ("core", "zh", "z0"))
    act, grad_out = activations.T, out_grad.T
    features, tokens = act.shape
    peer_out = lax.ppermute(grad_out, "zh", [(0, 1), (1, 0)])
    kept = lax.ppermute(momentum.T, COLUMN, TO_WORK)

    act, peer_out, kept = over_plane(act, (peer_out,), (kept,))
    act = act.reshape(X, Y, features, tokens)
    act = act.transpose(1, 0, 2, 3).reshape(ZL, -1, tokens)
    low_half = jnp.where(high == 0, grad_out, peer_out)
    high_half = jnp.where(high == 0, peer_out, grad_out)
    part = jnp.stack(
        [contract(half, act[k], ((1,), (1,))) for half in (low_half, high_half) for k in range(ZL)]
    )
    width, height = part.shape[1:]
    part = exchanged(part.reshape(CORES, ZL, width, height), "core").sum(axis=0)
    part = part.reshape(Z1, Z0, width, height).transpose(1, 0, 2, 3)
    part = exchanged(part, "z0").sum(axis=0)
    gradient = exchanged(part, "z1").sum(axis=0)

    new_momentum = 0.95 * kept + gradient
    scaled = (new_momentum / norm_scale).astype(jnp.bfloat16)
    momentum_home = lax.ppermute(new_momentum, COLUMN, TO_HOME)

    pair = lax.all_gather(scaled, "core", axis=0, tiled=True)
    panel, momentum_home = over_plane(scaled, (), (momentum_home,))
    depth = panel.shape[0]
    part = contract(panel, pair, ((1,), (1,)))
    piece = -(-depth // (2 * Z * 8)) * 8
    part = jnp.pad(part, ((0, 2 * Z * piece - depth), (0, 0)))
    part = part.reshape(2, Z0, Z // Z0 * piece, CORES * width)
    leaving = lax.dynamic_index_in_dim(part, 1 - odd, 1, False)
    staying = lax.dynamic_index_in_dim(part, odd, 1, False)
    came = jnp.stack(
        [lax.ppermute(leaving[0], NEAR, EVEN_PAIRS), lax.ppermute(leaving[1], NEAR, ODD_PAIRS)]
    )
    part = (staying + came).reshape(2, Z // Z0, piece, CORES * width).transpose(1, 0, 2, 3)
    gram = exchanged(part, ("zh", "z1")).sum(axis=0).astype(jnp.bfloat16)
    gram = lax.all_gather(gram, RING, axis=0, tiled=False).reshape(Z // Z0, Z0, 2, piece, CORES * width)
    gram = gram.transpose(2, 1, 0, 3, 4).reshape(-1, CORES * width)[:depth]

    def times_gram(rows):
        both = contract(gram, rows, ((0,), (0,))).reshape(CORES, width, height)
        both = lax.all_gather(both, "core", axis=0, tiled=False)
        return lax.dynamic_index_in_dim(both, core, 1, False).sum(axis=0)

    first_power = times_gram(panel).astype(jnp.bfloat16)
    second_power = times_gram(over_plane(first_power)[0])
    direction = (
        3.4445 * scaled.astype(jnp.float32)
        - 4.775 * first_power.astype(jnp.float32)
        + 2.0315 * second_power
    )
    direction = lax.ppermute(direction, COLUMN, TO_HOME).T
    factor = 0.2 * math.sqrt(max(ROWS, COLS))
    return (weight - step_size * factor * direction, momentum_home.T)


def solution(mesh):
    torus = Mesh(mesh.devices.reshape(Z1, Z0, CORES, ZH, Y, X), AXES)
    tiles = P(("z1", "z0", "core"), ("zh", "y", "x"))
    return jax.shard_map(
        per_device,
        mesh=torus,
        in_specs=(tiles, tiles, tiles, tiles, P(), P()),
        out_specs=(tiles, tiles),
        check_vma=False,
    )
```

```python
import itertools
import math

import jax
import jax.numpy as jnp
from jax import lax
from jax.experimental.layout import Layout, with_layout_constraint
from jax.sharding import Mesh
from jax.sharding import PartitionSpec as P

ROWS = 4224
COLS = 4096
Z1, Z0, CORES, ZH, Y, X = 3, 2, 2, 2, 8, 4
AXES = ("z1", "z0", "core", "zh", "y", "x")
COLUMN = ("z1", "z0", "core", "zh")
RING = ("zh", "z1", "z0")
NEAR = ("z1", "z0", "zh")
ZL, Z = Z1 * Z0, ZH * Z1 * Z0


def place(zl, core, zh):
    return (zl * CORES + core) * ZH + zh


def working_z(tile):
    return (tile // 2 + 3 + 6 * (tile % 2)) % Z


TO_WORK = [
    (place(tile // 2, tile % 2, half), place(working_z(tile) % ZL, half, working_z(tile) // ZL))
    for tile in range(Z)
    for half in range(CORES)
]
TO_HOME = [(work, home) for home, work in TO_WORK]


def dealt(turn):
    pairs = []
    for zl, core, zh, y, x in itertools.product(*map(range, (ZL, CORES, ZH, Y, X))):
        tile, unit = divmod(3 * ((zh * Y + y) * X + x) + (turn - zl) % 3, 16)
        to_zh, to_zl = divmod(working_z(tile), ZL)
        target = (place(to_zl, core, to_zh) * Y + unit % Y) * X + zl // 3 * 2 + unit // Y
        pairs.append(((place(zl, core, zh) * Y + y) * X + x, target))
    return pairs


def ring(z):
    return z % Z % ZL * ZH + z % Z // ZL


EVEN_PAIRS = [(ring(z), ring(z ^ 1)) for z in range(Z)]
ODD_PAIRS = [(ring(z), ring((z - 1 ^ 1) + 1)) for z in range(Z)]


def contract(left, right, dims):
    return lax.dot_general(left, right, (dims, ((), ())), preferred_element_type=jnp.float32)


def exchanged(pieces, axes):
    return lax.all_to_all(pieces, axes, split_axis=0, concat_axis=0, tiled=True)


def from_all(shard, axes, size):
    return exchanged(jnp.broadcast_to(shard[None], (size, *shard.shape)), axes)


def row_major(array):
    return with_layout_constraint(array, Layout(tuple(range(array.ndim))))


def over_plane(tile, beside_y=(), beside_x=()):
    rows, width = tile.shape
    by_y = from_all(tile, "y", Y).reshape(Y * rows, width)
    by_y, *beside_y = lax.optimization_barrier((row_major(by_y), *beside_y))
    panel = from_all(by_y, "x", X).reshape(X * Y * rows, width)
    panel, *beside_x = lax.optimization_barrier((row_major(panel), *beside_x))
    return panel, *beside_y, *beside_x


def per_device(activations, out_grad, momentum, weight, norm_scale, step_size):
    core, high, odd, y, x = (lax.axis_index(name) for name in ("core", "zh", "z0", "y", "x"))
    row_group = lax.axis_index("z1") * Z0 + odd
    act = activations.T.reshape(3, -1, activations.shape[0])
    kept = lax.ppermute(momentum.T, COLUMN, TO_WORK)

    hands = [
        lax.ppermute(lax.dynamic_index_in_dim(act, (turn + 2 * row_group) % 3, 0, False), AXES, dealt(turn))
        for turn in range(3)
    ]
    shift = (high * ZL + row_group + Z - 3) % Z
    tile = shift % 6 * 2 + shift // 6
    first = (tile + x % 2 * Y + y) % 3
    hands = lax.dynamic_slice_in_dim(jnp.stack(hands + hands[:2]), first, 3, 0)
    act = jnp.concatenate(list(hands), axis=1)
    grad_out = lax.all_gather(out_grad.T, RING, axis=0, tiled=False)
    act, grad_out, kept = over_plane(act, (grad_out,), (kept,))
    tokens = act.shape[1]
    act = act.reshape(2, -1, tokens)
    width, height = out_grad.shape[1], act.shape[1]
    grad_out = grad_out.reshape(ZH, ZL, width, -1).transpose(0, 2, 1, 3).reshape(ZH * width, -1)

    def own_columns(both):
        both = lax.all_gather(both.reshape(CORES, width, height), "core", axis=0, tiled=False)
        return lax.dynamic_index_in_dim(both, core, 1, False).sum(axis=0)

    gradient = own_columns(
        contract(grad_out[:, :tokens], act[0], ((1,), (1,)))
        + contract(grad_out[:, tokens:], act[1], ((1,), (1,)))
    )

    new_momentum = 0.95 * kept + gradient
    scaled = (new_momentum / norm_scale).astype(jnp.bfloat16)
    momentum_home = lax.ppermute(new_momentum, COLUMN, TO_HOME)

    pair = lax.all_gather(scaled, "core", axis=0, tiled=True)
    panel, momentum_home = over_plane(scaled, (), (momentum_home,))
    depth = panel.shape[0]
    part = contract(panel, pair, ((1,), (1,)))
    piece = -(-depth // (2 * Z * 8)) * 8
    part = jnp.pad(part, ((0, 2 * Z * piece - depth), (0, 0)))
    part = part.reshape(2, Z0, Z // Z0 * piece, CORES * width)
    leaving = lax.dynamic_index_in_dim(part, 1 - odd, 1, False)
    staying = lax.dynamic_index_in_dim(part, odd, 1, False)
    came = jnp.stack(
        [lax.ppermute(leaving[0], NEAR, EVEN_PAIRS), lax.ppermute(leaving[1], NEAR, ODD_PAIRS)]
    )
    part = (staying + came).reshape(2, Z // Z0, piece, CORES * width).transpose(1, 0, 2, 3)
    gram = exchanged(part, ("zh", "z1")).sum(axis=0).astype(jnp.bfloat16)
    gram = lax.all_gather(gram, RING, axis=0, tiled=False).reshape(Z // Z0, Z0, 2, piece, CORES * width)
    gram = gram.transpose(2, 1, 0, 3, 4).reshape(-1, CORES * width)[:depth]

    def times_gram(rows):
        return own_columns(contract(gram, rows, ((0,), (0,))))

    first_power = times_gram(panel).astype(jnp.bfloat16)
    second_power = times_gram(over_plane(first_power)[0])
    direction = (
        3.4445 * scaled.astype(jnp.float32)
        - 4.775 * first_power.astype(jnp.float32)
        + 2.0315 * second_power
    )
    direction = lax.ppermute(direction, COLUMN, TO_HOME).T
    factor = 0.2 * math.sqrt(max(ROWS, COLS))
    return (weight - step_size * factor * direction, momentum_home.T)


def solution(mesh):
    torus = Mesh(mesh.devices.reshape(Z1, Z0, CORES, ZH, Y, X), AXES)
    tiles = P(("z1", "z0", "core"), ("zh", "y", "x"))
    return jax.shard_map(
        per_device,
        mesh=torus,
        in_specs=(tiles, tiles, tiles, tiles, P(), P()),
        out_specs=(tiles, tiles),
        check_vma=False,
    )
```

```python
import math

import jax
import jax.numpy as jnp
from jax import lax
from jax.experimental.layout import Layout, with_layout_constraint
from jax.sharding import Mesh
from jax.sharding import PartitionSpec as P

ROWS = 4224
COLS = 4096
Z1, Z0, CORES, ZH, Y, X = 3, 2, 2, 2, 8, 4
AXES = ("z1", "z0", "core", "zh", "y", "x")
COLUMN = ("z1", "z0", "core", "zh")
RING = ("zh", "z1", "z0")
NEAR = ("z1", "z0", "zh")
ZL, Z = Z1 * Z0, ZH * Z1 * Z0


def place(zl, core, zh):
    return (zl * CORES + core) * ZH + zh


TO_WORK = [
    (place(3 * zh + zl // 2, zl % 2, core), place(zl, core, zh))
    for zl in range(ZL)
    for core in range(CORES)
    for zh in range(ZH)
]
TO_HOME = [(work, home) for home, work in TO_WORK]


def ring(z):
    return z % Z % ZL * ZH + z % Z // ZL


EVEN_PAIRS = [(ring(z), ring(z ^ 1)) for z in range(Z)]
ODD_PAIRS = [(ring(z), ring((z - 1 ^ 1) + 1)) for z in range(Z)]


def contract(left, right, dims):
    return lax.dot_general(left, right, (dims, ((), ())), preferred_element_type=jnp.float32)


def exchanged(pieces, axes):
    return lax.all_to_all(pieces, axes, split_axis=0, concat_axis=0, tiled=True)


def from_all(shard, axes, size):
    return exchanged(jnp.broadcast_to(shard[None], (size, *shard.shape)), axes)


def row_major(array):
    return with_layout_constraint(array, Layout(tuple(range(array.ndim))))


def over_y(tile, *beside):
    by_y = from_all(tile, "y", Y).reshape(-1, tile.shape[1])
    return lax.optimization_barrier((row_major(by_y), *beside))


def over_x(rows, *beside):
    panel = from_all(rows, "x", X).reshape(-1, rows.shape[1])
    return lax.optimization_barrier((row_major(panel), *beside))


def per_device(activations, out_grad, momentum, weight, norm_scale, step_size):
    odd = lax.axis_index("z0")
    act, grad_out = activations.T, out_grad.T
    features, tokens = act.shape
    halves = lax.all_gather(grad_out, "zh", axis=0, tiled=False)
    kept = lax.ppermute(momentum.T, COLUMN, TO_WORK)

    act, halves = over_y(act, halves)
    act, kept = over_x(act, kept)
    act = act.reshape(X, Y, features, tokens)
    act = act.transpose(1, 0, 2, 3).reshape(ZL, -1, tokens)
    part = jnp.stack(
        [contract(half, act[k], ((1,), (1,))) for half in halves for k in range(ZL)]
    )
    width, height = part.shape[1:]
    part = exchanged(part.reshape(CORES, ZL, width, height), "core").sum(axis=0)
    part = part.reshape(Z1, Z0, width, height).transpose(1, 0, 2, 3)
    part = exchanged(part, "z0").sum(axis=0)
    gradient = exchanged(part, "z1").sum(axis=0)

    new_momentum = 0.95 * kept + gradient
    scaled = (new_momentum / norm_scale).astype(jnp.bfloat16)
    momentum_home = lax.ppermute(new_momentum, COLUMN, TO_HOME)

    across = lax.all_gather(scaled, "core", axis=0, tiled=True)
    across = lax.all_gather(across, "x", axis=0, tiled=False)
    panel, across = over_y(scaled, across)
    part = jnp.einsum("br,kqr->kbq", panel, across, preferred_element_type=jnp.float32)
    part = part.reshape(-1, CORES * width)
    depth = part.shape[0]
    piece = -(-depth // (2 * Z * 8)) * 8
    part = jnp.pad(part, ((0, 2 * Z * piece - depth), (0, 0)))
    part = part.reshape(2, Z0, Z // Z0 * piece, CORES * width)
    leaving = lax.dynamic_index_in_dim(part, 1 - odd, 1, False)
    staying = lax.dynamic_index_in_dim(part, odd, 1, False)
    came = jnp.stack(
        [lax.ppermute(leaving[0], NEAR, EVEN_PAIRS), lax.ppermute(leaving[1], NEAR, ODD_PAIRS)]
    )
    part = (staying + came).reshape(2, Z // Z0, piece, CORES * width).transpose(1, 0, 2, 3)
    gram = exchanged(part, ("zh", "z1")).sum(axis=0).astype(jnp.bfloat16)
    gram = lax.all_gather(gram, RING, axis=0, tiled=False).reshape(Z // Z0, Z0, 2, piece, CORES * width)
    gram = gram.transpose(2, 1, 0, 3, 4).reshape(-1, CORES * width)[:depth]

    gram = gram.reshape(X, -1, CORES * width)

    def times_gram(rows):
        parts = jnp.einsum("kbq,br->kqr", gram, rows, preferred_element_type=jnp.float32)
        return exchanged(parts.reshape(-1, width, height), ("x", "core")).sum(axis=0)

    first_power = times_gram(panel).astype(jnp.bfloat16)
    panel, momentum_home = over_y(first_power, momentum_home)
    second_power = times_gram(panel)
    direction = (
        3.4445 * scaled.astype(jnp.float32)
        - 4.775 * first_power.astype(jnp.float32)
        + 2.0315 * second_power
    )
    direction = lax.ppermute(direction, COLUMN, TO_HOME).T
    factor = 0.2 * math.sqrt(max(ROWS, COLS))
    return (weight - step_size * factor * direction, momentum_home.T)


def solution(mesh):
    torus = Mesh(mesh.devices.reshape(Z1, Z0, CORES, ZH, Y, X), AXES)
    tiles = P(("z1", "z0", "core"), ("zh", "y", "x"))
    return jax.shard_map(
        per_device,
        mesh=torus,
        in_specs=(tiles, tiles, tiles, tiles, P(), P()),
        out_specs=(tiles, tiles),
        check_vma=False,
    )
```

```python
import math

import jax
import jax.numpy as jnp
from jax import lax
from jax.experimental.layout import Layout, with_layout_constraint
from jax.sharding import Mesh
from jax.sharding import PartitionSpec as P

ROWS = 4224
COLS = 4096
Z1, Z0, CORES, ZH, Y, X = 3, 2, 2, 2, 8, 4
AXES = ("z1", "z0", "core", "zh", "y", "x")
COLUMN = ("z1", "z0", "core", "zh")
RING = ("zh", "z1", "z0")
NEAR = ("z1", "z0", "zh")
ZL, Z = Z1 * Z0, ZH * Z1 * Z0


def place(zl, core, zh):
    return (zl * CORES + core) * ZH + zh


TO_WORK = [
    (place(3 * zh + zl // 2, zl % 2, core), place(zl, core, zh))
    for zl in range(ZL)
    for core in range(CORES)
    for zh in range(ZH)
]
TO_HOME = [(work, home) for home, work in TO_WORK]


def ring(z):
    return z % Z % ZL * ZH + z % Z // ZL


EVEN_PAIRS = [(ring(z), ring(z ^ 1)) for z in range(Z)]
ODD_PAIRS = [(ring(z), ring((z - 1 ^ 1) + 1)) for z in range(Z)]


def contract(left, right, dims):
    return lax.dot_general(left, right, (dims, ((), ())), preferred_element_type=jnp.float32)


def exchanged(pieces, axes):
    return lax.all_to_all(pieces, axes, split_axis=0, concat_axis=0, tiled=True)


def from_all(shard, axes, size):
    return exchanged(jnp.broadcast_to(shard[None], (size, *shard.shape)), axes)


def row_major(array):
    return with_layout_constraint(array, Layout(tuple(range(array.ndim))))


def over_y(tile, *beside):
    by_y = from_all(tile, "y", Y).reshape(-1, tile.shape[1])
    return lax.optimization_barrier((row_major(by_y), *beside))


def over_x(rows, *beside):
    panel = from_all(rows, "x", X).reshape(-1, rows.shape[1])
    return lax.optimization_barrier((row_major(panel), *beside))


def per_device(activations, out_grad, momentum, weight, norm_scale, step_size):
    odd = lax.axis_index("z0")
    act, grad_out = activations.T, out_grad.T
    features, tokens = act.shape
    halves = lax.all_gather(grad_out, "zh", axis=0, tiled=False)
    kept = lax.ppermute(momentum.T, COLUMN, TO_WORK)

    act, kept, halves = over_x(over_y(act)[0], kept, halves)
    act = act.reshape(X, Y, features, tokens)
    act = act.transpose(1, 0, 2, 3).reshape(ZL, -1, tokens)
    part = jnp.stack(
        [contract(half, act[k], ((1,), (1,))) for half in halves for k in range(ZL)]
    )
    width, height = part.shape[1:]
    part = exchanged(part.reshape(CORES, ZL, width, height), "core").sum(axis=0)
    part = part.reshape(Z1, Z0, width, height).transpose(1, 0, 2, 3)
    part = exchanged(part, "z0").sum(axis=0)
    gradient = exchanged(part, "z1").sum(axis=0)

    new_momentum = 0.95 * kept + gradient
    scaled = (new_momentum / norm_scale).astype(jnp.bfloat16)
    momentum_home = lax.ppermute(new_momentum, COLUMN, TO_HOME)

    across = lax.all_gather(scaled, "x", axis=0, tiled=True)
    panel, across = over_y(scaled, across)
    panel = lax.all_gather(panel, "core", axis=0, tiled=True)
    across = across.reshape(X // 2, 2 * width, height)
    part = jnp.einsum("br,kqr->kbq", panel, across, preferred_element_type=jnp.float32)
    part = part.reshape(-1, 2 * width)
    depth = part.shape[0]
    piece = -(-depth // (2 * Z * 8)) * 8
    part = jnp.pad(part, ((0, 2 * Z * piece - depth), (0, 0)))
    part = part.reshape(2, Z0, Z // Z0 * piece, 2 * width)
    leaving = lax.dynamic_index_in_dim(part, 1 - odd, 1, False)
    staying = lax.dynamic_index_in_dim(part, odd, 1, False)
    came = jnp.stack(
        [lax.ppermute(leaving[0], NEAR, EVEN_PAIRS), lax.ppermute(leaving[1], NEAR, ODD_PAIRS)]
    )
    part = (staying + came).reshape(2, Z // Z0, piece, 2 * width).transpose(1, 0, 2, 3)
    gram = exchanged(part, ("zh", "z1")).sum(axis=0).astype(jnp.bfloat16)
    gram = lax.all_gather(gram, RING, axis=0, tiled=False).reshape(Z // Z0, Z0, 2, piece, 2 * width)
    gram = gram.transpose(2, 1, 0, 3, 4).reshape(-1, 2 * width)[:depth]

    gram = gram.reshape(X // 2, -1, 2 * width)

    def times_gram(rows):
        parts = jnp.einsum("kbq,br->kqr", gram, rows, preferred_element_type=jnp.float32)
        return exchanged(parts.reshape(X, width, height), "x").sum(axis=0)

    first_power = times_gram(panel).astype(jnp.bfloat16)
    panel, momentum_home = over_y(first_power, momentum_home)
    second_power = times_gram(lax.all_gather(panel, "core", axis=0, tiled=True))
    direction = (
        3.4445 * scaled.astype(jnp.float32)
        - 4.775 * first_power.astype(jnp.float32)
        + 2.0315 * second_power
    )
    direction = lax.ppermute(direction, COLUMN, TO_HOME).T
    factor = 0.2 * math.sqrt(max(ROWS, COLS))
    return (weight - step_size * factor * direction, momentum_home.T)


def solution(mesh):
    torus = Mesh(mesh.devices.reshape(Z1, Z0, CORES, ZH, Y, X), AXES)
    tiles = P(("z1", "z0", "core"), ("zh", "y", "x"))
    return jax.shard_map(
        per_device,
        mesh=torus,
        in_specs=(tiles, tiles, tiles, tiles, P(), P()),
        out_specs=(tiles, tiles),
        check_vma=False,
    )
```

```python
import math

import jax
import jax.numpy as jnp
from jax import lax
from jax.experimental.layout import Layout, with_layout_constraint
from jax.sharding import Mesh
from jax.sharding import PartitionSpec as P

ROWS = 4224
COLS = 4096
Z1, Z0, CORES, ZH, Y, X = 3, 2, 2, 2, 8, 4
AXES = ("z1", "z0", "core", "zh", "y", "x")
COLUMN = ("z1", "z0", "core", "zh")
RING = ("zh", "z1", "z0")
NEAR = ("z1", "z0", "zh")
ZL, Z = Z1 * Z0, ZH * Z1 * Z0


def place(zl, core, zh):
    return (zl * CORES + core) * ZH + zh


TO_WORK = [
    (place(3 * zh + zl // 2, zl % 2, core), place(zl, core, zh))
    for zl in range(ZL)
    for core in range(CORES)
    for zh in range(ZH)
]
TO_HOME = [(work, home) for home, work in TO_WORK]


def ring(z):
    return z % Z % ZL * ZH + z % Z // ZL


EVEN_PAIRS = [(ring(z), ring(z ^ 1)) for z in range(Z)]
ODD_PAIRS = [(ring(z), ring((z - 1 ^ 1) + 1)) for z in range(Z)]


def contract(left, right, dims):
    return lax.dot_general(left, right, (dims, ((), ())), preferred_element_type=jnp.float32)


def exchanged(pieces, axes):
    return lax.all_to_all(pieces, axes, split_axis=0, concat_axis=0, tiled=True)


def from_all(shard, axes, size):
    return exchanged(jnp.broadcast_to(shard[None], (size, *shard.shape)), axes)


def row_major(array):
    return with_layout_constraint(array, Layout(tuple(range(array.ndim))))


def over_y(tile, *beside):
    by_y = from_all(tile, "y", Y).reshape(-1, tile.shape[1])
    return lax.optimization_barrier((row_major(by_y), *beside))


def over_x(rows, *beside):
    panel = from_all(rows, "x", X).reshape(-1, rows.shape[1])
    return lax.optimization_barrier((row_major(panel), *beside))


def per_device(activations, out_grad, momentum, weight, norm_scale, step_size):
    odd = lax.axis_index("z0")
    act, grad_out = activations.T, out_grad.T
    features, tokens = act.shape
    halves = lax.all_gather(grad_out, "zh", axis=0, tiled=False)
    kept = lax.ppermute(momentum.T, COLUMN, TO_WORK)

    act, halves = over_x(over_y(act)[0], halves)
    act = act.reshape(X, Y, features, tokens)
    act = act.transpose(1, 0, 2, 3).reshape(ZL, -1, tokens)
    part = jnp.einsum("cqk,grk->cgqr", halves, act, preferred_element_type=jnp.float32)
    width, height = part.shape[2:]
    part = exchanged(part, "core").sum(axis=0)
    part = part.reshape(Z1, Z0, width, height).transpose(1, 0, 2, 3)
    part = exchanged(part, "z0").sum(axis=0)
    gradient = exchanged(part, "z1").sum(axis=0)

    new_momentum = 0.95 * kept + gradient
    scaled = (new_momentum / norm_scale).astype(jnp.bfloat16)
    momentum_home = lax.ppermute(new_momentum, COLUMN, TO_HOME)

    across = lax.all_gather(scaled, "x", axis=0, tiled=True)
    panel, across = over_y(scaled, across)
    panel = lax.all_gather(panel, "core", axis=0, tiled=True)
    across = across.reshape(X // 2, 2 * width, height)
    part = jnp.einsum("br,kqr->kbq", panel, across, preferred_element_type=jnp.float32)
    part = part.reshape(-1, 2 * width)
    depth = part.shape[0]
    piece = -(-depth // (2 * Z * 8)) * 8
    part = jnp.pad(part, ((0, 2 * Z * piece - depth), (0, 0)))
    part = part.reshape(2, Z0, Z // Z0 * piece, 2 * width)
    leaving = lax.dynamic_index_in_dim(part, 1 - odd, 1, False)
    staying = lax.dynamic_index_in_dim(part, odd, 1, False)
    came = jnp.stack(
        [lax.ppermute(leaving[0], NEAR, EVEN_PAIRS), lax.ppermute(leaving[1], NEAR, ODD_PAIRS)]
    )
    part = (staying + came).reshape(2, Z // Z0, piece, 2 * width).transpose(1, 0, 2, 3)
    gram = exchanged(part, ("z1", "zh")).sum(axis=0).astype(jnp.bfloat16)
    gram = lax.all_gather(gram, RING, axis=0, tiled=False).reshape(ZH, Z1, Z0, 2, piece, 2 * width)
    gram = gram.transpose(3, 2, 1, 0, 4, 5).reshape(-1, 2 * width)[:depth]
    gram = gram.reshape(X // 2, -1, 2 * width)

    def times_gram(rows):
        parts = jnp.einsum("kbq,br->kqr", gram, rows, preferred_element_type=jnp.float32)
        return exchanged(parts.reshape(X, width, height), "x").sum(axis=0)

    first_power = times_gram(panel).astype(jnp.bfloat16)
    panel, momentum_home = over_y(first_power, momentum_home)
    second_power = times_gram(lax.all_gather(panel, "core", axis=0, tiled=True))
    direction = (
        3.4445 * scaled.astype(jnp.float32)
        - 4.775 * first_power.astype(jnp.float32)
        + 2.0315 * second_power
    )
    direction = lax.ppermute(direction, COLUMN, TO_HOME).T
    factor = 0.2 * math.sqrt(max(ROWS, COLS))
    return (weight - step_size * factor * direction, momentum_home.T)


def solution(mesh):
    torus = Mesh(mesh.devices.reshape(Z1, Z0, CORES, ZH, Y, X), AXES)
    tiles = P(("z1", "z0", "core"), ("zh", "y", "x"))
    return jax.shard_map(
        per_device,
        mesh=torus,
        in_specs=(tiles, tiles, tiles, tiles, P(), P()),
        out_specs=(tiles, tiles),
        check_vma=False,
    )
```

```python
import math

import jax
import jax.numpy as jnp
from jax import lax
from jax.experimental.layout import Layout, with_layout_constraint
from jax.sharding import Mesh
from jax.sharding import PartitionSpec as P

ROWS = 4224
COLS = 4096
Z1, Z0, CORES, ZH, Y, X = 3, 2, 2, 2, 8, 4
AXES = ("z1", "z0", "core", "zh", "y", "x")
COLUMN = ("z1", "z0", "core", "zh")
RING = ("zh", "z1", "z0")
NEAR = ("z1", "z0", "zh")
ZL, Z = Z1 * Z0, ZH * Z1 * Z0


def place(zl, core, zh):
    return (zl * CORES + core) * ZH + zh


TO_WORK = [
    (place(3 * zh + zl // 2, zl % 2, core), place(zl, core, zh))
    for zl in range(ZL)
    for core in range(CORES)
    for zh in range(ZH)
]
TO_HOME = [(work, home) for home, work in TO_WORK]


def ring(z):
    return z % Z % ZL * ZH + z % Z // ZL


EVEN_PAIRS = [(ring(z), ring(z ^ 1)) for z in range(Z)]
ODD_PAIRS = [(ring(z), ring((z - 1 ^ 1) + 1)) for z in range(Z)]


def contract(left, right, dims):
    return lax.dot_general(left, right, (dims, ((), ())), preferred_element_type=jnp.float32)


def exchanged(pieces, axes):
    return lax.all_to_all(pieces, axes, split_axis=0, concat_axis=0, tiled=True)


def from_all(shard, axes, size):
    return exchanged(jnp.broadcast_to(shard[None], (size, *shard.shape)), axes)


def row_major(array):
    return with_layout_constraint(array, Layout(tuple(range(array.ndim))))


def over_y(tile, *beside):
    by_y = from_all(tile, "y", Y).reshape(-1, tile.shape[1])
    return lax.optimization_barrier((row_major(by_y), *beside))


def over_x(rows, *beside):
    panel = from_all(rows, "x", X).reshape(-1, rows.shape[1])
    return lax.optimization_barrier((row_major(panel), *beside))


def per_device(activations, out_grad, momentum, weight, norm_scale, step_size):
    odd = lax.axis_index("z0")
    act, grad_out = activations.T, out_grad.T
    features, tokens = act.shape
    halves = lax.all_gather(grad_out, "zh", axis=0, tiled=False)
    kept = lax.ppermute(momentum.T, COLUMN, TO_WORK)

    act, halves = over_x(over_y(act)[0], halves)
    act = act.reshape(X, Y, features, tokens)
    act = act.transpose(1, 0, 2, 3).reshape(ZL, -1, tokens)
    part = jnp.einsum("cqk,grk->cgqr", halves, act, preferred_element_type=jnp.float32)
    width, height = part.shape[2:]
    part = exchanged(part, "core").sum(axis=0)
    part = part.reshape(Z1, Z0, width, height).transpose(1, 0, 2, 3)
    leaving = lax.dynamic_index_in_dim(part, 1 - odd, 0, False)
    part = lax.dynamic_index_in_dim(part, odd, 0, False)
    part += lax.ppermute(leaving, "z0", [(0, 1), (1, 0)])
    third = lax.axis_index("z1")
    gradient = lax.dynamic_index_in_dim(part, third, 0, False)
    for ahead in range(1, Z1):
        leaving = lax.dynamic_index_in_dim(part, (third + ahead) % Z1, 0, False)
        gradient += lax.ppermute(leaving, "z1", [(k, (k + ahead) % Z1) for k in range(Z1)])

    new_momentum = 0.95 * kept + gradient
    scaled = (new_momentum / norm_scale).astype(jnp.bfloat16)
    momentum_home = lax.ppermute(new_momentum, COLUMN, TO_HOME)

    across = lax.all_gather(scaled, "x", axis=0, tiled=True)
    panel, across = over_y(scaled, across)
    panel = lax.all_gather(panel, "core", axis=0, tiled=True)
    across = across.reshape(X // 2, 2 * width, height)
    part = jnp.einsum("br,kqr->kbq", panel, across, preferred_element_type=jnp.float32)
    part = part.reshape(-1, 2 * width)
    depth = part.shape[0]
    piece = -(-depth // (2 * Z * 8)) * 8
    part = jnp.pad(part, ((0, 2 * Z * piece - depth), (0, 0)))
    part = part.reshape(2, Z0, Z // Z0 * piece, 2 * width)
    leaving = lax.dynamic_index_in_dim(part, 1 - odd, 1, False)
    staying = lax.dynamic_index_in_dim(part, odd, 1, False)
    came = jnp.stack(
        [lax.ppermute(leaving[0], NEAR, EVEN_PAIRS), lax.ppermute(leaving[1], NEAR, ODD_PAIRS)]
    )
    part = (staying + came).reshape(2, Z // Z0, piece, 2 * width).transpose(1, 0, 2, 3)
    gram = exchanged(part, ("z1", "zh")).sum(axis=0).astype(jnp.bfloat16)
    gram = lax.all_gather(gram, RING, axis=0, tiled=False).reshape(ZH, Z1, Z0, 2, piece, 2 * width)
    gram = gram.transpose(3, 2, 1, 0, 4, 5).reshape(-1, 2 * width)[:depth]
    gram = gram.reshape(X // 2, -1, 2 * width)

    def times_gram(rows):
        parts = jnp.einsum("kbq,br->kqr", gram, rows, preferred_element_type=jnp.float32)
        return exchanged(parts.reshape(X, width, height), "x").sum(axis=0)

    first_power = times_gram(panel).astype(jnp.bfloat16)
    panel, momentum_home = over_y(first_power, momentum_home)
    second_power = times_gram(lax.all_gather(panel, "core", axis=0, tiled=True))
    direction = (
        3.4445 * scaled.astype(jnp.float32)
        - 4.775 * first_power.astype(jnp.float32)
        + 2.0315 * second_power
    )
    direction = lax.ppermute(direction, COLUMN, TO_HOME).T
    factor = 0.2 * math.sqrt(max(ROWS, COLS))
    return (weight - step_size * factor * direction, momentum_home.T)


def solution(mesh):
    torus = Mesh(mesh.devices.reshape(Z1, Z0, CORES, ZH, Y, X), AXES)
    tiles = P(("z1", "z0", "core"), ("zh", "y", "x"))
    return jax.shard_map(
        per_device,
        mesh=torus,
        in_specs=(tiles, tiles, tiles, tiles, P(), P()),
        out_specs=(tiles, tiles),
        check_vma=False,
    )
```

```python
import math

import jax
import jax.numpy as jnp
from jax import lax
from jax.experimental.layout import Layout, with_layout_constraint
from jax.sharding import Mesh
from jax.sharding import PartitionSpec as P

ROWS = 4224
COLS = 4096
Z1, Z0, CORES, ZH, Y, X = 3, 2, 2, 2, 8, 4
AXES = ("z1", "z0", "core", "zh", "y", "x")
COLUMN = ("z1", "z0", "core", "zh")
RING = ("zh", "z1", "z0")
NEAR = ("z1", "z0", "zh")
ZL, Z = Z1 * Z0, ZH * Z1 * Z0


def place(zl, core, zh):
    return (zl * CORES + core) * ZH + zh


TO_WORK = [
    (place(3 * zh + zl // 2, zl % 2, core), place(zl, core, zh))
    for zl in range(ZL)
    for core in range(CORES)
    for zh in range(ZH)
]
TO_HOME = [(work, home) for home, work in TO_WORK]


def ring(z):
    return z % Z % ZL * ZH + z % Z // ZL


EVEN_PAIRS = [(ring(z), ring(z ^ 1)) for z in range(Z)]
ODD_PAIRS = [(ring(z), ring((z - 1 ^ 1) + 1)) for z in range(Z)]


def contract(left, right, dims):
    return lax.dot_general(left, right, (dims, ((), ())), preferred_element_type=jnp.float32)


def exchanged(pieces, axes):
    return lax.all_to_all(pieces, axes, split_axis=0, concat_axis=0, tiled=True)


def from_all(shard, axes, size):
    return exchanged(jnp.broadcast_to(shard[None], (size, *shard.shape)), axes)


def row_major(array):
    return with_layout_constraint(array, Layout(tuple(range(array.ndim))))


def over_y(tile, *beside):
    by_y = from_all(tile, "y", Y).reshape(-1, tile.shape[1])
    return lax.optimization_barrier((row_major(by_y), *beside))


def over_x(rows, *beside):
    panel = from_all(rows, "x", X).reshape(-1, rows.shape[1])
    return lax.optimization_barrier((row_major(panel), *beside))


def per_device(activations, out_grad, momentum, weight, norm_scale, step_size):
    odd = lax.axis_index("z0")
    act, grad_out = activations.T, out_grad.T
    features, tokens = act.shape
    halves = lax.all_gather(grad_out, "zh", axis=0, tiled=False)
    kept = lax.ppermute(momentum.T, COLUMN, TO_WORK)

    act, halves = over_x(over_y(act)[0], halves)
    act = act.reshape(X, Y, features, tokens)
    act = act.transpose(1, 0, 2, 3).reshape(ZL, -1, tokens)
    part = jnp.einsum("cqk,grk->cgqr", halves, act, preferred_element_type=jnp.float32)
    width, height = part.shape[2:]
    part = exchanged(part, "core").sum(axis=0)
    part = part.reshape(Z1, Z0, width, height).transpose(1, 0, 2, 3)
    leaving = lax.dynamic_index_in_dim(part, 1 - odd, 0, False)
    part = lax.dynamic_index_in_dim(part, odd, 0, False)
    part += lax.ppermute(leaving, "z0", [(0, 1), (1, 0)])
    third = lax.axis_index("z1")
    gradient = lax.dynamic_index_in_dim(part, third, 0, False)
    for ahead in range(1, Z1):
        leaving = lax.dynamic_index_in_dim(part, (third + ahead) % Z1, 0, False)
        gradient += lax.ppermute(leaving, "z1", [(k, (k + ahead) % Z1) for k in range(Z1)])

    new_momentum = 0.95 * kept + gradient
    scaled = (new_momentum / norm_scale).astype(jnp.bfloat16)
    momentum_home = lax.ppermute(new_momentum, COLUMN, TO_HOME)

    across = lax.all_gather(scaled, "x", axis=0, tiled=True)
    panel, across = over_y(scaled, across)
    panel = lax.all_gather(panel, "core", axis=0, tiled=True)
    across = across.reshape(X // 2, 2 * width, height)
    part = jnp.einsum("br,kqr->kbq", panel, across, preferred_element_type=jnp.float32)
    part = part.reshape(-1, 2 * width)
    depth = part.shape[0]
    piece = -(-depth // (2 * Z * 8)) * 8
    part = jnp.pad(part, ((0, 2 * Z * piece - depth), (0, 0)))
    part = part.reshape(2, Z0, Z // Z0 * piece, 2 * width)
    leaving = lax.dynamic_index_in_dim(part, 1 - odd, 1, False)
    staying = lax.dynamic_index_in_dim(part, odd, 1, False)
    came = (lax.ppermute(leaving[0], NEAR, EVEN_PAIRS), lax.ppermute(leaving[1], NEAR, ODD_PAIRS))
    shape = (Z // Z0, 1, piece, 2 * width)
    part = jnp.concatenate([(staying[k] + came[k]).reshape(shape) for k in range(2)], axis=1)
    gram = exchanged(part, ("z1", "zh")).sum(axis=0).astype(jnp.bfloat16)
    gram = lax.all_gather(gram, RING, axis=0, tiled=False).reshape(ZH, Z1, Z0, 2, piece, 2 * width)
    gram = gram.transpose(3, 2, 1, 0, 4, 5).reshape(-1, 2 * width)[:depth]
    gram = gram.reshape(X // 2, -1, 2 * width)

    def times_gram(rows):
        parts = jnp.einsum("kbq,br->kqr", gram, rows, preferred_element_type=jnp.float32)
        return exchanged(parts.reshape(X, width, height), "x").sum(axis=0)

    first_power = times_gram(panel).astype(jnp.bfloat16)
    panel, momentum_home = over_y(first_power, momentum_home)
    second_power = times_gram(lax.all_gather(panel, "core", axis=0, tiled=True))
    direction = (
        3.4445 * scaled.astype(jnp.float32)
        - 4.775 * first_power.astype(jnp.float32)
        + 2.0315 * second_power
    )
    direction = lax.ppermute(direction, COLUMN, TO_HOME).T
    factor = 0.2 * math.sqrt(max(ROWS, COLS))
    return (weight - step_size * factor * direction, momentum_home.T)


def solution(mesh):
    torus = Mesh(mesh.devices.reshape(Z1, Z0, CORES, ZH, Y, X), AXES)
    tiles = P(("z1", "z0", "core"), ("zh", "y", "x"))
    return jax.shard_map(
        per_device,
        mesh=torus,
        in_specs=(tiles, tiles, tiles, tiles, P(), P()),
        out_specs=(tiles, tiles),
        check_vma=False,
    )
```
